512 devices in a mesh: tm: 64 (over z, y), head: 8 (over x, core).
Axes of the slice: x: 4, y: 8, z: 8, core: 2. Of those that a mesh axis runs over, the one named last changes fastest.
Arguments:
- queries: bfloat16 [10240, 3072], P('tm', 'head'), may hold values from -200 to 200
- keys: bfloat16 [10240, 3072], P('tm', 'head'), may hold values from -8 to 8
- values: bfloat16 [10240, 3072], P('tm', 'head'), may hold values from -6 to 6
- block_group: int32 [64], replicated, may hold values from 0 to 3, as said below
- group_mask: int32 [4, 4], replicated, may hold values from 0 to 1, as said below
- teacher_gain: float32 [3072], P('head'), may hold values from 0.25 to 1.75
Outputs:
- student_out: bfloat16 [10240, 3072], P('tm', 'head')
- teacher_out: bfloat16 [10240, 3072], P('tm', 'head')
- gap: float32 [10240], P('tm')
The draws below stay inside these ranges and needn't reach their ends.
Inputs may be any that keep to these rules, and one draw needn't show every extreme that they name: `block_group`: never falls from one block to the next, starts at 0 and ends at 3; every group holds one block or more. `group_mask`: entry (i, j) is 1 where j == i or j == i - 1, 0 where j > i; the other entries are 0 or 1.
All inputs are finite; a program needn't handle non-finite values.
Results may differ from the reference program's by a relative error of at most 0.0095.
Values may be sent and summed in bfloat16 or wider, within the bound.
A program may use at most 128 MiB of HBM per device.

```python
import jax
import jax.numpy as jnp
from jax import lax

HD = 128
HEADS = 24
NCHUNK = 4
TOK_DEV = 160
TOKENS = 10240
NBLK = 64


def draw_queries(key, part):
    key = jax.random.fold_in(key, 3)
    return jnp.clip(jax.random.normal(key, (TOKENS, HEADS * HD), jnp.float32), -6.0, 6.0).astype(jnp.bfloat16)


def draw_keys(key, part):
    key = jax.random.fold_in(key, 4)
    return jnp.clip(jax.random.normal(key, (TOKENS, HEADS * HD), jnp.float32), -6.0, 6.0).astype(jnp.bfloat16)


def draw_block_group(key, part):
    key = jax.random.fold_in(key, 5)
    cuts = jnp.sort(jax.random.permutation(key, NBLK - 1)[:NCHUNK - 1] + 1)
    positions = jnp.arange(NBLK, dtype=jnp.int32)
    return jnp.sum((positions[:, None] >= cuts[None, :]).astype(jnp.int32), axis=1).astype(jnp.int32)


def draw_group_mask(key, part):
    key = jax.random.fold_in(key, 6)
    random_bits = jax.random.randint(key, (NCHUNK, NCHUNK), 0, 2, jnp.int32)
    row_index = jnp.arange(NCHUNK, dtype=jnp.int32)[:, None]
    col_index = jnp.arange(NCHUNK, dtype=jnp.int32)[None, :]
    forced = (col_index == row_index) | (col_index == row_index - 1)
    lower = col_index < row_index
    return jnp.where(forced, 1, jnp.where(lower, random_bits, 0)).astype(jnp.int32)


def block_levels(own_key, shape, shards, smallest, top_value):
    def one(position, parts):
        draws = jax.random.uniform(jax.random.fold_in(jax.random.fold_in(own_key, 6), position), (parts,), jnp.float32, smallest / len(shards), top_value / len(shards))
        return jnp.repeat(jnp.exp(draws), shape[position] // parts).reshape((-1,) + (1,) * (len(shape) - position - 1))

    gain = one(*shards[0])
    for cut in shards[1:]:
        gain = gain * one(*cut)
    return gain


def scatter_about(key, dims, width, most, shards=(), held_as=jnp.bfloat16):
    values = width * jax.random.normal(key, dims, jnp.float32)
    if shards:
        values = values * block_levels(key, dims, shards, -0.22, 0.18)
    return jnp.clip(values, -most, most).astype(held_as)


def setup_inputs(seed: int = 0) -> dict:
    key_list = jax.random.split(jax.random.key(seed), 7)
    queries = draw_queries(jax.random.fold_in(key_list[6], 71), 0)
    keys = draw_keys(jax.random.fold_in(key_list[6], 71), 0)
    values = scatter_about(key_list[2], (TOKENS, HEADS * HD), 1.0, 6.0, ((0, 64), (1, 8)))
    block_group = draw_block_group(jax.random.fold_in(key_list[6], 71), 0)
    group_mask = draw_group_mask(jax.random.fold_in(key_list[6], 71), 0)
    teacher_gain = jnp.clip(1.0 + 0.15 * jax.random.normal(key_list[5], (HEADS * HD,), jnp.float32), 0.25, 1.75)
    return {"queries": queries, "keys": keys, "values": values, "block_group": block_group, "group_mask": group_mask, "teacher_gain": teacher_gain}


def attend(query_head, key_head, value_head, permitted):
    scores = jnp.dot(query_head, key_head.T, preferred_element_type=jnp.float32) * (HD ** -0.5)
    scores = jnp.where(permitted, scores, jnp.float32(-1e30))
    largest = jnp.max(scores, axis=-1, keepdims=True)
    weights = jnp.where(permitted, jnp.exp(scores - largest), jnp.float32(0.0))
    denom = jnp.sum(weights, axis=-1, keepdims=True)
    mixed = jnp.dot(weights.astype(jnp.bfloat16), value_head, preferred_element_type=jnp.float32) / denom
    return mixed.astype(jnp.bfloat16)


def reference(queries, keys, values, block_group, group_mask, teacher_gain):
    token_count = queries.shape[0]
    group_of = block_group[jnp.arange(token_count) // TOK_DEV]
    student_keep = group_mask[group_of[:, None], group_of[None, :]] == 1
    teacher_keep = jnp.ones((token_count, token_count), dtype=bool)
    teacher_q = (queries.astype(jnp.float32) * teacher_gain[None, :]).astype(jnp.bfloat16)

    def split_heads(array):
        return array.reshape(token_count, HEADS, HD).transpose(1, 0, 2)

    def join_heads(array):
        return array.transpose(1, 0, 2).reshape(token_count, HEADS * HD)

    def per_head(operands):
        student_head, teacher_head, key_head, value_head = operands
        return (attend(student_head, key_head, value_head, student_keep),
                attend(teacher_head, key_head, value_head, teacher_keep))

    student, teacher = lax.map(per_head, (split_heads(queries), split_heads(teacher_q), split_heads(keys), split_heads(values)))
    student_out = join_heads(student)
    teacher_out = join_heads(teacher)
    difference = teacher_out.astype(jnp.float32) - student_out.astype(jnp.float32)
    gap = jnp.mean(difference * difference, axis=-1)
    return student_out, teacher_out, gap
```

```python
import functools
import math

import jax
import jax.numpy as jnp
from jax import lax
from jax.experimental import pallas as pl
from jax.experimental.pallas import tpu as pltpu
from jax.sharding import PartitionSpec as P

HD = 128
RING = 8
HEADS_DEV = 3
PEERS = 8
ROWS = 160
STAT = 16
KEYS = RING * ROWS
UNITS = RING * HEADS_DEV
SCALE = math.log2(math.e) / math.sqrt(HD)
EMPTY = -1e30
MESH = pl.DeviceIdType.MESH
NT = (((1,), (1,)), ((), ()))
TN = (((0,), (0,)), ((), ()))
BF = jnp.bfloat16
F32 = jnp.float32


def kernel(
    q_ref, k_ref, v_ref, group_ref, mask_ref, gain_ref,
    s_out, t_out, gap_out,
    k_all, v_all, q_all, bias, gains, score0, score1, part, lse, inbox, outbox, gap_sum, gap_in,
    g_send, g_recv, o_send, o_recv, d_send, d_recv,
):
    tm = lax.axis_index("tm")
    head = lax.axis_index("head")
    core = lax.rem(head, 2)
    zpos, ypos = lax.div(tm, RING), lax.rem(tm, RING)
    kpos = jnp.where(core == 0, zpos, ypos)
    qpos = jnp.where(core == 0, ypos, zpos)

    def device(kp, qp):
        return jnp.where(core == 0, kp * RING + qp, qp * RING + kp)

    def wrap(x):
        return lax.rem(x + 2 * RING, RING)

    k_near = {1: device(wrap(kpos + 1), qpos), -1: device(wrap(kpos - 1), qpos)}
    q_near = {1: device(kpos, wrap(qpos + 1)), -1: device(kpos, wrap(qpos - 1))}

    barrier = pltpu.get_barrier_semaphore()
    for near in (*k_near.values(), *q_near.values()):
        pl.semaphore_signal(barrier, inc=1, device_id={"tm": near}, device_id_type=MESH)
    for step in range(1, PEERS):
        pl.semaphore_signal(
            barrier, inc=1, device_id={"head": lax.rem(head + step, PEERS)}, device_id_type=MESH
        )

    own = {"k": k_ref, "v": v_ref, "q": q_ref}
    whole = {"k": k_all, "v": v_all, "q": q_all}
    position = {"k": kpos, "v": kpos, "q": qpos}
    nearby = {"k": k_near, "v": k_near, "q": q_near}
    legs = [(name, way, hop) for name in "kvq" for way in (1, -1) for hop in range(1, 4)]
    legs += [("k", 1, 4), ("v", -1, 4), ("q", 1, 4)]
    slot = {leg: number for number, leg in enumerate(legs)}

    def leg_copy(h, leg, arriving):
        name, way, hop = leg
        block = wrap(position[name] - way * (hop if arriving else hop - 1))
        there = whole[name].at[h, block]
        if hop == 1 and not arriving:
            here = own[name].at[:, pl.ds(h * HD, HD)]
        else:
            here = there
        return pltpu.make_async_remote_copy(
            src_ref=here,
            dst_ref=there,
            send_sem=g_send.at[h, slot[leg]],
            recv_sem=g_recv.at[h, slot[leg]],
            device_id={"tm": nearby[name][way]},
            device_id_type=MESH,
        )

    def send_hop(h, hop):
        for leg in legs:
            if leg[2] == hop:
                leg_copy(h, leg, False).start()

    def wait_hop(h, hop):
        for leg in legs:
            if leg[2] == hop:
                leg_copy(h, leg, True).wait_recv()

    def relay(h, hop):
        for leg in legs:
            if leg[2] == hop:
                leg_copy(h, leg, True).wait_recv()
                onward = (leg[0], leg[1], hop + 1)
                if onward in slot:
                    leg_copy(h, onward, False).start()

    def place(j):
        return wrap(qpos + jnp.where(lax.rem(j, 2) == 1, lax.div(7 - j, 2), lax.div(j + 8, 2)))

    pl.semaphore_wait(barrier, 4 + PEERS - 1)
    send_hop(0, 1)
    send_hop(1, 1)

    for h in range(HEADS_DEV):
        columns = slice(h * HD, (h + 1) * HD)
        k_all[h, kpos] = k_ref[:, columns]
        v_all[h, kpos] = v_ref[:, columns]
        q_all[h, qpos] = q_ref[:, columns]
        gains[h] = jnp.broadcast_to(gain_ref[columns][None, :], (8, HD))
        for first in range(2):
            inbox[h, first, :ROWS, :] = jnp.zeros((ROWS, 2 * HD), BF)
            stat_row = lax.broadcasted_iota(jnp.int32, (STAT, 2 * HD), 0)
            inbox[h, first, ROWS:, :] = jnp.where(
                (stat_row == 0) | (stat_row == 3), F32(EMPTY), F32(0.0)
            ).astype(BF)
    gap_sum[...] = jnp.zeros((ROWS, HD), F32)

    def set_bias(j, carry):
        q_group = group_ref[device(kpos, place(j))]
        block_of = lax.div(lax.broadcasted_iota(jnp.int32, (8, KEYS), 1), ROWS)
        row = jnp.zeros((8, KEYS), F32)
        for b in range(RING):
            keep = mask_ref[q_group, group_ref[device(b, qpos)]]
            row = jnp.where(block_of == b, jnp.where(keep == 1, F32(0.0), F32(EMPTY)), row)
        bias[j] = row
        return carry

    lax.fori_loop(0, RING, set_bias, 0)

    relay(0, 1)
    relay(1, 1)
    relay(0, 2)
    relay(1, 2)
    send_hop(2, 1)
    relay(0, 3)
    relay(1, 3)
    wait_hop(0, 4)

    def scores(h, j, score):
        queries = q_all[h, place(j)]
        gain = gains[h][0:1, :]
        teacher = (queries.astype(F32) * gain).astype(BF)
        both = jnp.concatenate([queries, teacher], axis=0)
        keys = k_all[h].reshape(KEYS, HD)
        score[...] = lax.dot_general(both, keys, NT, preferred_element_type=F32)

    def mix(h, j, score):
        s = jnp.concatenate([score[:ROWS, :] + bias[j][0:1, :], score[ROWS:, :]], axis=0)
        largest = jnp.max(s, axis=-1, keepdims=True)
        weight = jnp.exp2((s - largest) * SCALE).astype(BF)
        right = jnp.concatenate(
            [v_all[h].reshape(KEYS, HD), jnp.ones((KEYS, HD), BF)], axis=1
        )
        mixed = jnp.dot(weight, right, preferred_element_type=F32)
        denom = mixed[:, HD:]
        part[h, j] = mixed[:, :HD] / denom
        lse[h, j] = largest * SCALE + jnp.log2(denom)

    def unit(u):
        later = u - RING
        h = jnp.where(u < RING, 0, 1 + lax.rem(later + 2, 2))
        j = jnp.where(u < RING, u, lax.div(later, 2))
        return h, j

    stat_lane = lax.broadcasted_iota(jnp.int32, (ROWS, HD), 1)
    pick = lax.broadcasted_iota(jnp.int32, (STAT, HD), 0)
    diagonal = (pick == lax.broadcasted_iota(jnp.int32, (STAT, HD), 1)).astype(F32).astype(BF)
    spread = [
        ((pick >= 3 * i) & (pick < 3 * i + 3)).astype(F32).astype(BF) for i in range(2)
    ]

    def merge(h, box, i, out, log):
        came = inbox[h, box, :ROWS, i * HD:(i + 1) * HD].astype(F32)
        stat = inbox[h, box, ROWS:, :]
        came_log = lax.dot_general(stat, spread[i], TN, preferred_element_type=F32)[:ROWS]
        ahead = log - came_log
        share = 1.0 / (1.0 + jnp.exp2(ahead))
        return (
            out + share * (came - out),
            jnp.maximum(log, came_log) + jnp.log2(1.0 + jnp.exp2(-jnp.abs(ahead))),
        )

    def message(h, j, way, arriving):
        box = inbox.at[h, j + 2]
        return pltpu.make_async_remote_copy(
            src_ref=box if arriving else outbox.at[h, j],
            dst_ref=box,
            send_sem=o_send.at[h, j],
            recv_sem=o_recv.at[h, j],
            device_id={"tm": jnp.where(lax.rem(j, 2) == 1, q_near[1], q_near[-1])},
            device_id_type=MESH,
        )

    def pass_on(h, j):
        @pl.when(j >= 2)
        def _():
            message(h, j - 2, None, True).wait_recv()

        packed = jnp.zeros((ROWS, HD), F32)
        for i in range(2):
            out, log = merge(
                h, j, i, part[h, j, i * ROWS:(i + 1) * ROWS, :], lse[h, j, i * ROWS:(i + 1) * ROWS, :]
            )
            outbox[h, j, :ROWS, i * HD:(i + 1) * HD] = out.astype(BF)
            rest = log
            for piece in range(3):
                rounded = rest.astype(BF).astype(F32)
                packed = jnp.where(stat_lane == 3 * i + piece, rounded, packed)
                rest = rest - rounded
        packed = jnp.concatenate([packed, jnp.zeros((2 * HD - ROWS, HD), F32)], axis=0).astype(BF)
        outbox[h, j, ROWS:, :] = lax.dot_general(
            diagonal, packed, NT, preferred_element_type=F32
        ).astype(BF)
        message(h, j, None, False).start()

    def work(g, last=False):
        u = 2 * g
        h0, j0 = unit(u)
        h1, j1 = unit(u + 1)
        scores(h1, j1, score1)
        mix(h0, j0, score0)
        if not last:
            h2, j2 = unit(u + 2)
            scores(h2, j2, score0)
        mix(h1, j1, score1)

    scores(0, 0, score0)

    def turn(g, carry):
        for when, hop in ((0, 1), (1, 2), (2, 3)):
            @pl.when(g == when)
            def _(hop=hop):
                relay(2, hop)

        @pl.when(g == 3)
        def _():
            wait_hop(1, 4)
            wait_hop(2, 4)

        work(g)

        @pl.when((g >= 2) & (g <= 8))
        def _():
            pass_on(0, g - 2)

        @pl.when(g >= 4)
        def _():
            pass_on(1, g - 4)
            pass_on(2, g - 4)

        return carry

    lax.fori_loop(0, UNITS // 2 - 1, turn, 0)
    work(jnp.int32(UNITS // 2 - 1), last=True)

    for h in range(HEADS_DEV):
        message(h, 5, None, True).wait_recv()
        message(h, 6, None, True).wait_recv()
        final = []
        for i in range(2):
            out, log = merge(
                h, 7, i,
                part[h, 7, i * ROWS:(i + 1) * ROWS, :], lse[h, 7, i * ROWS:(i + 1) * ROWS, :],
            )
            out, log = merge(h, 8, i, out, log)
            final.append(out.astype(BF))
        s_out[:, h * HD:(h + 1) * HD] = final[0]
        t_out[:, h * HD:(h + 1) * HD] = final[1]
        apart = final[1].astype(F32) - final[0].astype(F32)
        gap_sum[...] += apart * apart

    tall = jnp.concatenate([gap_sum[...], jnp.zeros((2 * HD - ROWS, HD), F32)], axis=0)
    gap_in[head] = lax.dot_general(
        jnp.ones((8, HD), F32), tall, NT, preferred_element_type=F32,
        precision=lax.Precision.HIGHEST,
    )

    def gap_copy(step, arriving):
        other = lax.rem(head + (PEERS - step if arriving else step), PEERS)
        box = gap_in.at[other if arriving else head]
        return pltpu.make_async_remote_copy(
            src_ref=box,
            dst_ref=box,
            send_sem=d_send.at[step - 1],
            recv_sem=d_recv.at[step - 1],
            device_id={"head": other},
            device_id_type=MESH,
        )

    for step in range(1, PEERS):
        gap_copy(step, False).start()
    for h in range(HEADS_DEV):
        for leg in legs:
            leg_copy(h, leg, False).wait_send()
        for j in range(RING - 1):
            message(h, j, None, False).wait_send()
    for step in range(1, PEERS):
        gap_copy(step, True).wait_recv()
    total = gap_in[0]
    for peer in range(1, PEERS):
        total = total + gap_in[peer]
    gap_out[...] = total / F32(PEERS * HEADS_DEV * HD)
    for step in range(1, PEERS):
        gap_copy(step, False).wait_send()


def on_device(queries, keys, values, block_group, group_mask, teacher_gain):
    vmem = pl.BlockSpec(memory_space=pltpu.VMEM)
    smem = pl.BlockSpec(memory_space=pltpu.SMEM)
    legs = 21
    student, teacher, gap = pl.pallas_call(
        kernel,
        out_shape=(
            jax.ShapeDtypeStruct((ROWS, HEADS_DEV * HD), BF),
            jax.ShapeDtypeStruct((ROWS, HEADS_DEV * HD), BF),
            jax.ShapeDtypeStruct((8, 2 * HD), F32),
        ),
        in_specs=[vmem, vmem, vmem, smem, smem, vmem],
        out_specs=(vmem, vmem, vmem),
        scratch_shapes=[
            pltpu.VMEM((HEADS_DEV, RING, ROWS, HD), BF),
            pltpu.VMEM((HEADS_DEV, RING, ROWS, HD), BF),
            pltpu.VMEM((HEADS_DEV, RING, ROWS, HD), BF),
            pltpu.VMEM((RING, 8, KEYS), F32),
            pltpu.VMEM((HEADS_DEV, 8, HD), F32),
            pltpu.VMEM((2 * ROWS, KEYS), F32),
            pltpu.VMEM((2 * ROWS, KEYS), F32),
            pltpu.VMEM((HEADS_DEV, RING, 2 * ROWS, HD), F32),
            pltpu.VMEM((HEADS_DEV, RING, 2 * ROWS, HD), F32),
            pltpu.VMEM((HEADS_DEV, RING + 1, ROWS + STAT, 2 * HD), BF),
            pltpu.VMEM((HEADS_DEV, RING - 1, ROWS + STAT, 2 * HD), BF),
            pltpu.VMEM((ROWS, HD), F32),
            pltpu.VMEM((PEERS, 8, 2 * HD), F32),
            pltpu.SemaphoreType.DMA((HEADS_DEV, legs)),
            pltpu.SemaphoreType.DMA((HEADS_DEV, legs)),
            pltpu.SemaphoreType.DMA((HEADS_DEV, RING - 1)),
            pltpu.SemaphoreType.DMA((HEADS_DEV, RING - 1)),
            pltpu.SemaphoreType.DMA((PEERS - 1,)),
            pltpu.SemaphoreType.DMA((PEERS - 1,)),
        ],
        compiler_params=pltpu.CompilerParams(
            collective_id=0, has_side_effects=True, vmem_limit_bytes=48 * 2**20
        ),
    )(queries, keys, values, block_group, group_mask, teacher_gain)
    return student, teacher, gap[0, :ROWS]


def solution(mesh):
    placed = (P("tm", "head"), P("tm", "head"), P("tm", "head"), P(), P(), P("head"))
    return jax.shard_map(
        on_device,
        mesh=mesh,
        in_specs=placed,
        out_specs=(P("tm", "head"), P("tm", "head"), P("tm")),
        check_vma=False,
    )
```

```python
import functools
import math

import jax
import jax.numpy as jnp
from jax import lax
from jax.experimental import pallas as pl
from jax.experimental.pallas import tpu as pltpu
from jax.sharding import PartitionSpec as P

HD = 128
RING = 8
HEADS_DEV = 3
PEERS = 8
ROWS = 160
STAT = 16
KEYS = RING * ROWS
UNITS = RING * HEADS_DEV
SCALE = math.log2(math.e) / math.sqrt(HD)
EMPTY = -(2.0**100)
MESH = pl.DeviceIdType.MESH
NT = (((1,), (1,)), ((), ()))
TN = (((0,), (0,)), ((), ()))
BF = jnp.bfloat16
F32 = jnp.float32


def kernel(
    q_ref, k_ref, v_ref, group_ref, mask_ref, gain_ref,
    s_out, t_out, gap_out,
    kv_all, q_all, group_all, mask_all, gain_all, bias, gains, score0, score1, inbox, outbox, gap_sum, gap_in,
    l_sem, g_send, g_recv, o_send, o_recv, d_send, d_recv,
):
    tm = lax.axis_index("tm")
    head = lax.axis_index("head")
    core = lax.rem(head, 2)
    zpos, ypos = lax.div(tm, RING), lax.rem(tm, RING)
    kpos = jnp.where(core == 0, zpos, ypos)
    qpos = jnp.where(core == 0, ypos, zpos)

    def device(kp, qp):
        return jnp.where(core == 0, kp * RING + qp, qp * RING + kp)

    def wrap(x):
        return lax.rem(x + 2 * RING, RING)

    def k_device(shift):
        return device(wrap(kpos + shift), qpos)

    def q_device(shift):
        return device(kpos, wrap(qpos + shift))

    sources = (q_ref, k_ref, v_ref)
    own_copies = []
    for h in range(HEADS_DEV):
        places = (q_all.at[0, h], kv_all.at[h, 0, 0], kv_all.at[h, 0, 1])
        for i, (source, place) in enumerate(zip(sources, places)):
            own_copies.append(
                pltpu.make_async_copy(source.at[:, pl.ds(h * HD, HD)], place, l_sem.at[h, i])
            )
    small = ((group_ref, group_all), (mask_ref, mask_all), (gain_ref, gain_all))
    small_copies = [
        pltpu.make_async_copy(source, place, l_sem.at[HEADS_DEV, i])
        for i, (source, place) in enumerate(small)
    ]
    for copy in own_copies + small_copies:
        copy.start()

    barrier = pltpu.get_barrier_semaphore()
    nears = [k_device(1), k_device(-1)] + [q_device(shift) for shift in (1, -1, 2, -2)]
    for near in nears:
        pl.semaphore_signal(barrier, inc=1, device_id={"tm": near}, device_id_type=MESH)
    for step in range(1, PEERS):
        pl.semaphore_signal(
            barrier, inc=1, device_id={"head": lax.rem(head + step, PEERS)}, device_id_type=MESH
        )

    def number(way, far):
        return 0 if far == 0 else 7 if far == 4 else 2 * far - (way > 0)

    def offset(k):
        return jnp.where(lax.rem(k, 2) == 1, lax.div(k + 1, 2), -lax.div(k, 2))

    legs = [(what, way, hop) for hop in (1, 2, 3) for what in (0, "q", 1, 2) for way in (1, -1)]
    legs += [(0, 1, 4), (0, -1, 4), ("q", 1, 4), (1, 1, 4), (1, -1, 4), (2, 1, 4), (2, -1, 4)]

    def leg_copy(leg):
        what, way, hop = leg
        here, there = number(-way, hop - 1), number(-way, hop)
        if what == "q":
            ends = q_all.at[here], q_all.at[there]
            near = q_device(way)
        else:
            ends = kv_all.at[what, here], kv_all.at[what, there]
            if hop == 4:
                half = 0 if way == 1 else 1
                ends = tuple(end.at[half] for end in ends)
            near = k_device(way)
        i = legs.index(leg)
        return pltpu.make_async_remote_copy(
            src_ref=ends[0],
            dst_ref=ends[1],
            send_sem=g_send.at[i],
            recv_sem=g_recv.at[i],
            device_id={"tm": near},
            device_id_type=MESH,
        )

    def relay(hop):
        for leg in legs:
            if leg[2] == hop:
                leg_copy(leg).wait_recv()
                onward = (leg[0], leg[1], hop + 1)
                if onward in legs:
                    leg_copy(onward).start()

    def wait_last(what):
        for leg in legs:
            if leg[0] == what and leg[2] == 4:
                leg_copy(leg).wait_recv()

    pl.semaphore_wait(barrier, len(nears) + PEERS - 1)
    for copy in own_copies:
        copy.wait()
    for leg in legs:
        if leg[2] == 1:
            leg_copy(leg).start()

    for copy in small_copies:
        copy.wait()
    for h in range(HEADS_DEV):
        gains[h] = jnp.broadcast_to(gain_all[h * HD:(h + 1) * HD][None, :], (8, HD))
    gap_sum[...] = jnp.zeros((ROWS, HD), F32)

    def set_bias(k, carry):
        q_group = group_all[device(kpos, wrap(qpos + offset(k)))]
        block_of = lax.div(lax.broadcasted_iota(jnp.int32, (8, KEYS), 1), ROWS)
        row = jnp.zeros((8, KEYS), F32)
        for i in range(RING):
            step = (i + 1) // 2 if i % 2 else -(i // 2)
            keep = mask_all[q_group, group_all[k_device(step)]]
            row = jnp.where(block_of == i, jnp.where(keep == 1, F32(0.0), F32(EMPTY)), row)
        bias[k] = row
        return carry

    lax.fori_loop(0, RING, set_bias, 0)

    for hop in (1, 2, 3):
        relay(hop)
    wait_last(0)

    def scores(h, k, score):
        queries = q_all[k, h]
        gain = gains[h][0:1, :]
        teacher = (queries.astype(F32) * gain).astype(BF)
        both = jnp.concatenate([queries, teacher], axis=0)
        keys = kv_all[h, :, 0].reshape(KEYS, HD)
        score[...] = lax.dot_general(both, keys, NT, preferred_element_type=F32)

    def mix(h, k, score):
        s = jnp.concatenate([score[:ROWS, :] + bias[k][0:1, :], score[ROWS:, :]], axis=0)
        shift = jnp.max(s, axis=-1, keepdims=True).astype(BF).astype(F32)
        weight = jnp.exp2((s - shift) * SCALE).astype(BF)
        right = jnp.concatenate(
            [kv_all[h, :, 1].reshape(KEYS, HD), jnp.ones((KEYS, HD), BF)], axis=1
        )
        mixed = jnp.dot(weight, right, preferred_element_type=F32)
        shift = jnp.broadcast_to(shift, (2 * ROWS, HD))
        halves = (slice(0, ROWS), slice(ROWS, 2 * ROWS))
        pack(h, k, [(mixed[half, :HD], shift[half], mixed[half, HD:]) for half in halves])

    def unit(u):
        v = u - 7
        h = jnp.where(
            v < 0, 0,
            jnp.where(
                v >= 14, v - 14,
                jnp.where((v < 3) | (v == 6) | (v == 7) | (v == 10) | (v == 11), 1, 2),
            ),
        )
        k = jnp.where(
            v < 0, u + 1,
            jnp.where(
                v >= 14, 0,
                jnp.where(v < 3, 7 - v, jnp.where(v < 8, 10 - v, jnp.where(v < 12, 12 - v, 14 - v))),
            ),
        )
        return h, k

    stat_lane = lax.broadcasted_iota(jnp.int32, (ROWS, HD), 1)
    stat_row = lax.broadcasted_iota(jnp.int32, (STAT, 2 * HD), 0)
    sum_side = jnp.where(lax.broadcasted_iota(jnp.int32, (STAT, 2 * HD), 1) >= HD, 1, 0)
    wanted = [lax.div(stat_row - 3 * i + 1, 2) for i in range(2)]
    spread = [
        jnp.where((wanted[i] == sum_side) & (stat_row >= 3 * i), F32(1.0), F32(0.0)).astype(BF)
        for i in range(2)
    ]

    def unpack(box, h, k, i):
        out = box[h, k, :ROWS, i * HD:(i + 1) * HD].astype(F32)
        stat = lax.dot_general(
            box[h, k, ROWS:, :], spread[i], TN, preferred_element_type=F32
        )[:ROWS]
        return out, stat[:, :HD], stat[:, HD:]

    def merge(parts):
        top = parts[0][1]
        for _, shift, _ in parts[1:]:
            top = jnp.maximum(top, shift)
        mixed = 0.0
        total = 0.0
        for out, shift, weight in parts:
            share = jnp.exp2((shift - top) * SCALE)
            mixed = mixed + share * out
            total = total + share * weight
        return mixed, top, total

    def message(h, k, shift):
        return pltpu.make_async_remote_copy(
            src_ref=outbox.at[h, k],
            dst_ref=inbox.at[h, k],
            send_sem=o_send.at[h, k],
            recv_sem=o_recv.at[h, k],
            device_id={"tm": q_device(shift)},
            device_id_type=MESH,
        )

    def arrived(h, k):
        message(h, k, 1).wait_recv()

    def pack(h, k, parts):
        packed = jnp.zeros((ROWS, HD), F32)
        for i, (out, shift, weight) in enumerate(parts):
            outbox[h, k, :ROWS, i * HD:(i + 1) * HD] = out.astype(BF)
            upper = weight.astype(BF).astype(F32)
            for piece, value in enumerate((shift, upper, weight - upper)):
                packed = jnp.where(stat_lane == 3 * i + piece, value, packed)
        packed = jnp.concatenate([packed, jnp.zeros((2 * HD - ROWS, HD), F32)], axis=0)
        outbox[h, k, ROWS:, :] = packed.T[:STAT].astype(BF)

    def pass_on(h, k, shift, others):
        for other in others:
            arrived(h, other)
        pack(h, k, [
            merge([unpack(outbox, h, k, i)] + [unpack(inbox, h, other, i) for other in others])
            for i in range(2)
        ])
        message(h, k, shift).start()

    def work(g, last=False):
        h0, k0 = unit(2 * g)
        h1, k1 = unit(2 * g + 1)
        scores(h1, k1, score1)
        mix(h0, k0, score0)
        if not last:
            h2, k2 = unit(2 * g + 2)
            scores(h2, k2, score0)
        mix(h1, k1, score1)
        return (h0, k0), (h1, k1)

    scores(0, 1, score0)

    def turn(g, carry):
        for when, what in ((2, "q"), (3, 1), (4, 2)):
            @pl.when(g == when)
            def _(what=what):
                wait_last(what)

        done = work(g)
        for h, k in done:
            @pl.when((k != 0) & (k != 3) & (k != 4))
            def _(h=h, k=k):
                message(h, k, jnp.where(k == 7, 2, jnp.where(lax.rem(k, 2) == 1, 1, -1))).start()

        @pl.when((g == 5) | (g == 7) | (g == 8))
        def _():
            pass_on(jnp.where(g == 5, 0, g - 6), 4, -2, (6,))

        @pl.when((g == 6) | (g == 7) | (g == 9))
        def _():
            pass_on(jnp.where(g == 6, 0, jnp.where(g == 7, 1, 2)), 3, 2, (5, 7))

        return carry

    lax.fori_loop(0, UNITS // 2 - 1, turn, 0)
    work(jnp.int32(UNITS // 2 - 1), last=True)

    for h in range(HEADS_DEV):
        for k in (1, 2, 3, 4):
            arrived(h, k)
        final = []
        for i in range(2):
            out, _, total = merge(
                [unpack(outbox, h, 0, i)] + [unpack(inbox, h, k, i) for k in (1, 2, 3, 4)]
            )
            final.append((out / total).astype(BF))
        s_out[:, h * HD:(h + 1) * HD] = final[0]
        t_out[:, h * HD:(h + 1) * HD] = final[1]
        apart = final[1].astype(F32) - final[0].astype(F32)
        gap_sum[...] += apart * apart

    tall = jnp.concatenate([gap_sum[...], jnp.zeros((2 * HD - ROWS, HD), F32)], axis=0)
    gap_in[head] = jnp.broadcast_to(jnp.sum(tall.T, axis=0, keepdims=True), (8, 2 * HD))

    def gap_copy(step, arriving):
        other = lax.rem(head + (PEERS - step if arriving else step), PEERS)
        box = gap_in.at[other if arriving else head]
        return pltpu.make_async_remote_copy(
            src_ref=box,
            dst_ref=box,
            send_sem=d_send.at[step - 1],
            recv_sem=d_recv.at[step - 1],
            device_id={"head": other},
            device_id_type=MESH,
        )

    for step in range(1, PEERS):
        gap_copy(step, False).start()
    for leg in legs:
        leg_copy(leg).wait_send()
    for h in range(HEADS_DEV):
        for k in range(1, RING):
            message(h, k, 1).wait_send()
    for step in range(1, PEERS):
        gap_copy(step, True).wait_recv()
    total = gap_in[0]
    for peer in range(1, PEERS):
        total = total + gap_in[peer]
    gap_out[...] = total / F32(PEERS * HEADS_DEV * HD)
    for step in range(1, PEERS):
        gap_copy(step, False).wait_send()


def on_device(queries, keys, values, block_group, group_mask, teacher_gain):
    vmem = pl.BlockSpec(memory_space=pltpu.VMEM)
    outside = pl.BlockSpec(memory_space=pltpu.HBM)
    legs = 31
    student, teacher, gap = pl.pallas_call(
        kernel,
        out_shape=(
            jax.ShapeDtypeStruct((ROWS, HEADS_DEV * HD), BF),
            jax.ShapeDtypeStruct((ROWS, HEADS_DEV * HD), BF),
            jax.ShapeDtypeStruct((8, 2 * HD), F32),
        ),
        in_specs=[outside] * 6,
        out_specs=(vmem, vmem, vmem),
        scratch_shapes=[
            pltpu.VMEM((HEADS_DEV, RING, 2, ROWS, HD), BF),
            pltpu.VMEM((RING, HEADS_DEV, ROWS, HD), BF),
            pltpu.SMEM(block_group.shape, jnp.int32),
            pltpu.SMEM(group_mask.shape, jnp.int32),
            pltpu.VMEM(teacher_gain.shape, F32),
            pltpu.VMEM((RING, 8, KEYS), F32),
            pltpu.VMEM((HEADS_DEV, 8, HD), F32),
            pltpu.VMEM((2 * ROWS, KEYS), F32),
            pltpu.VMEM((2 * ROWS, KEYS), F32),
            pltpu.VMEM((HEADS_DEV, RING, ROWS + STAT, 2 * HD), BF),
            pltpu.VMEM((HEADS_DEV, RING, ROWS + STAT, 2 * HD), BF),
            pltpu.VMEM((ROWS, HD), F32),
            pltpu.VMEM((PEERS, 8, 2 * HD), F32),
            pltpu.SemaphoreType.DMA((HEADS_DEV + 1, 3)),
            pltpu.SemaphoreType.DMA((legs,)),
            pltpu.SemaphoreType.DMA((legs,)),
            pltpu.SemaphoreType.DMA((HEADS_DEV, RING)),
            pltpu.SemaphoreType.DMA((HEADS_DEV, RING)),
            pltpu.SemaphoreType.DMA((PEERS - 1,)),
            pltpu.SemaphoreType.DMA((PEERS - 1,)),
        ],
        compiler_params=pltpu.CompilerParams(
            collective_id=0, has_side_effects=True, vmem_limit_bytes=64 * 2**20
        ),
    )(queries, keys, values, block_group, group_mask, teacher_gain)
    return student, teacher, gap[0, :ROWS]


def solution(mesh):
    placed = (P("tm", "head"), P("tm", "head"), P("tm", "head"), P(), P(), P("head"))
    return jax.shard_map(
        on_device,
        mesh=mesh,
        in_specs=placed,
        out_specs=(P("tm", "head"), P("tm", "head"), P("tm")),
        check_vma=False,
    )
```

```python
import functools
import math

import jax
import jax.numpy as jnp
from jax import lax
from jax.experimental import pallas as pl
from jax.experimental.pallas import tpu as pltpu
from jax.sharding import PartitionSpec as P

HD = 128
RING = 8
HEADS_DEV = 3
PEERS = 8
ROWS = 160
STAT = 16
KEYS = RING * ROWS
UNITS = RING * HEADS_DEV
SCALE = math.log2(math.e) / math.sqrt(HD)
EMPTY = -(2.0**100)
MESH = pl.DeviceIdType.MESH
NT = (((1,), (1,)), ((), ()))
TN = (((0,), (0,)), ((), ()))
BF = jnp.bfloat16
F32 = jnp.float32


def kernel(
    q_ref, k_ref, v_ref, group_ref, mask_ref, gain_ref,
    s_hbm, t_hbm, gap_hbm,
    kv_all, q_all, group_all, mask_all, gain_all, bias, gains, score0, score1, s_out, t_out, gap_out, inbox, outbox, gap_sum, gap_in,
    l_sem, w_sem, g_send, g_recv, o_send, o_recv, d_send, d_recv,
):
    tm = lax.axis_index("tm")
    head = lax.axis_index("head")
    core = lax.rem(head, 2)
    zpos, ypos = lax.div(tm, RING), lax.rem(tm, RING)
    kpos = jnp.where(core == 0, zpos, ypos)
    qpos = jnp.where(core == 0, ypos, zpos)

    def device(kp, qp):
        return jnp.where(core == 0, kp * RING + qp, qp * RING + kp)

    def wrap(x):
        return lax.rem(x + 2 * RING, RING)

    def k_device(shift):
        return device(wrap(kpos + shift), qpos)

    def q_device(shift):
        return device(kpos, wrap(qpos + shift))

    sources = (q_ref, k_ref, v_ref)
    own_copies = []
    for h in range(HEADS_DEV):
        places = (q_all.at[0, h], kv_all.at[h, 0, 0], kv_all.at[h, 0, 1])
        for i, (source, place) in enumerate(zip(sources, places)):
            own_copies.append(
                pltpu.make_async_copy(source.at[:, pl.ds(h * HD, HD)], place, l_sem.at[h, i])
            )
    small = ((group_ref, group_all), (mask_ref, mask_all), (gain_ref, gain_all))
    small_copies = [
        pltpu.make_async_copy(source, place, l_sem.at[HEADS_DEV, i])
        for i, (source, place) in enumerate(small)
    ]
    for copy in own_copies + small_copies:
        copy.start()

    barrier = pltpu.get_barrier_semaphore()
    nears = [k_device(1), k_device(-1)] + [q_device(shift) for shift in (1, -1, 2, -2)]
    for near in nears:
        pl.semaphore_signal(barrier, inc=1, device_id={"tm": near}, device_id_type=MESH)
    for step in range(1, PEERS):
        pl.semaphore_signal(
            barrier, inc=1, device_id={"head": lax.rem(head + step, PEERS)}, device_id_type=MESH
        )

    def number(way, far):
        return 0 if far == 0 else 7 if far == 4 else 2 * far - (way > 0)

    def offset(k):
        return jnp.where(lax.rem(k, 2) == 1, lax.div(k + 1, 2), -lax.div(k, 2))

    legs = [(what, way, hop) for hop in (1, 2, 3) for what in (0, "q", 1, 2) for way in (1, -1)]
    legs += [(0, 1, 4), (0, -1, 4), ("q", 1, 4), (1, 1, 4), (1, -1, 4), (2, 1, 4), (2, -1, 4)]

    def leg_copy(leg):
        what, way, hop = leg
        here, there = number(-way, hop - 1), number(-way, hop)
        if what == "q":
            ends = q_all.at[here], q_all.at[there]
            near = q_device(way)
        else:
            ends = kv_all.at[what, here], kv_all.at[what, there]
            if hop == 4:
                half = 0 if way == 1 else 1
                ends = tuple(end.at[half] for end in ends)
            near = k_device(way)
        i = legs.index(leg)
        return pltpu.make_async_remote_copy(
            src_ref=ends[0],
            dst_ref=ends[1],
            send_sem=g_send.at[i],
            recv_sem=g_recv.at[i],
            device_id={"tm": near},
            device_id_type=MESH,
        )

    def send_own(leg):
        what, way, _ = leg
        i = legs.index(leg)
        if what == "q":
            pieces = [(q_ref, h, q_all.at[number(-way, 1), h]) for h in range(HEADS_DEV)]
        else:
            pieces = [
                (source, what, kv_all.at[what, number(-way, 1), half])
                for half, source in enumerate((k_ref, v_ref))
            ]
        for source, h, place in pieces:
            pltpu.make_async_remote_copy(
                src_ref=source.at[:, pl.ds(h * HD, HD)],
                dst_ref=place,
                send_sem=g_send.at[i],
                recv_sem=g_recv.at[i],
                device_id={"tm": (q_device if what == "q" else k_device)(way)},
                device_id_type=MESH,
            ).start()

    def relay(hop):
        for leg in legs:
            if leg[2] == hop:
                leg_copy(leg).wait_recv()
                onward = (leg[0], leg[1], hop + 1)
                if onward in legs:
                    leg_copy(onward).start()

    def wait_last(what):
        for leg in legs:
            if leg[0] == what and leg[2] == 4:
                leg_copy(leg).wait_recv()

    pl.semaphore_wait(barrier, len(nears) + PEERS - 1)
    for leg in legs:
        if leg[2] == 1:
            send_own(leg)

    for copy in small_copies:
        copy.wait()
    for h in range(HEADS_DEV):
        gains[h] = jnp.broadcast_to(gain_all[h * HD:(h + 1) * HD][None, :], (8, HD))
    gap_sum[...] = jnp.zeros((ROWS, HD), F32)

    def set_bias(k, carry):
        q_group = group_all[device(kpos, wrap(qpos + offset(k)))]
        block_of = lax.div(lax.broadcasted_iota(jnp.int32, (8, KEYS), 1), ROWS)
        row = jnp.zeros((8, KEYS), F32)
        for i in range(RING):
            step = (i + 1) // 2 if i % 2 else -(i // 2)
            keep = mask_all[q_group, group_all[k_device(step)]]
            row = jnp.where(block_of == i, jnp.where(keep == 1, F32(0.0), F32(EMPTY)), row)
        bias[k] = row
        return carry

    lax.fori_loop(0, RING, set_bias, 0)

    for copy in own_copies:
        copy.wait()
    for hop in (1, 2, 3):
        relay(hop)
    wait_last(0)

    def scores(h, k, score):
        queries = q_all[k, h]
        gain = gains[h][0:1, :]
        teacher = (queries.astype(F32) * gain).astype(BF)
        both = jnp.concatenate([queries, teacher], axis=0)
        keys = kv_all[h, :, 0].reshape(KEYS, HD)
        score[...] = lax.dot_general(both, keys, NT, preferred_element_type=F32)

    def mix(h, k, score):
        s = jnp.concatenate([score[:ROWS, :] + bias[k][0:1, :], score[ROWS:, :]], axis=0)
        shift = jnp.max(s, axis=-1, keepdims=True).astype(BF).astype(F32)
        weight = jnp.exp2((s - shift) * SCALE).astype(BF)
        right = jnp.concatenate(
            [kv_all[h, :, 1].reshape(KEYS, HD), jnp.ones((KEYS, HD), BF)], axis=1
        )
        mixed = jnp.dot(weight, right, preferred_element_type=F32)
        shift = jnp.broadcast_to(shift, (2 * ROWS, HD))
        halves = (slice(0, ROWS), slice(ROWS, 2 * ROWS))
        pack(h, k, [(mixed[half, :HD], shift[half], mixed[half, HD:]) for half in halves])

    def unit(u):
        far = u - 3
        middle = u - 9
        near = u - 15
        last = lax.rem(far + 3, 3)
        h = jnp.where(
            u < 3, 0,
            jnp.where(
                u < 9, 1 + lax.div(far, 3),
                jnp.where(u < 15, lax.div(middle, 2), jnp.where(u < 21, lax.div(near, 2), u - 21)),
            ),
        )
        k = jnp.where(
            u < 3, 5 + u,
            jnp.where(
                u < 9, jnp.where(last == 0, 7, 4 + last),
                jnp.where(
                    u < 15, 3 + lax.rem(middle, 2), jnp.where(u < 21, 1 + lax.rem(near, 2), 0)
                ),
            ),
        )
        return h, k

    stat_lane = lax.broadcasted_iota(jnp.int32, (ROWS, HD), 1)
    stat_row = lax.broadcasted_iota(jnp.int32, (STAT, 2 * HD), 0)
    sum_side = jnp.where(lax.broadcasted_iota(jnp.int32, (STAT, 2 * HD), 1) >= HD, 1, 0)
    wanted = [lax.div(stat_row - 3 * i + 1, 2) for i in range(2)]
    spread = [
        jnp.where((wanted[i] == sum_side) & (stat_row >= 3 * i), F32(1.0), F32(0.0)).astype(BF)
        for i in range(2)
    ]

    def unpack(box, h, k, i):
        out = box[h, k, :ROWS, i * HD:(i + 1) * HD].astype(F32)
        stat = lax.dot_general(
            box[h, k, ROWS:, :], spread[i], TN, preferred_element_type=F32
        )[:ROWS]
        return out, stat[:, :HD], stat[:, HD:]

    def merge(parts):
        top = parts[0][1]
        for _, shift, _ in parts[1:]:
            top = jnp.maximum(top, shift)
        mixed = 0.0
        total = 0.0
        for out, shift, weight in parts:
            share = jnp.exp2((shift - top) * SCALE)
            mixed = mixed + share * out
            total = total + share * weight
        return mixed, top, total

    def message(h, k, shift):
        return pltpu.make_async_remote_copy(
            src_ref=outbox.at[h, k],
            dst_ref=inbox.at[h, k],
            send_sem=o_send.at[h, k],
            recv_sem=o_recv.at[h, k],
            device_id={"tm": q_device(shift)},
            device_id_type=MESH,
        )

    def arrived(h, k):
        message(h, k, 1).wait_recv()

    def pack(h, k, parts):
        packed = jnp.zeros((ROWS, HD), F32)
        for i, (out, shift, weight) in enumerate(parts):
            outbox[h, k, :ROWS, i * HD:(i + 1) * HD] = out.astype(BF)
            upper = weight.astype(BF).astype(F32)
            for piece, value in enumerate((shift, upper, weight - upper)):
                packed = jnp.where(stat_lane == 3 * i + piece, value, packed)
        packed = jnp.concatenate([packed, jnp.zeros((2 * HD - ROWS, HD), F32)], axis=0)
        outbox[h, k, ROWS:, :] = packed.T[:STAT].astype(BF)

    def pass_on(h, k, shift, others):
        for other in others:
            arrived(h, other)
        pack(h, k, [
            merge([unpack(outbox, h, k, i)] + [unpack(inbox, h, other, i) for other in others])
            for i in range(2)
        ])
        message(h, k, shift).start()

    def work(g, last=False):
        h0, k0 = unit(2 * g)
        h1, k1 = unit(2 * g + 1)
        scores(h1, k1, score1)
        mix(h0, k0, score0)
        if not last:
            h2, k2 = unit(2 * g + 2)
            scores(h2, k2, score0)
        mix(h1, k1, score1)
        return (h0, k0), (h1, k1)

    scores(0, 5, score0)

    joins = ((3, (5,), 4, (0, 2)), (3, (5, 7), 4, (1,)), (4, (6, 7), 5, (0, 2)), (4, (6,), 5, (1,)))
    joins += ((1, (3,), 7, (0, 1, 2)), (2, (4,), 8, (0, 1, 2)))

    def turn(g, carry):
        for when, what in ((0, "q"), (1, 1), (2, 2)):
            @pl.when(g == when)
            def _(what=what):
                wait_last(what)

        for h, k in work(g):
            @pl.when(k >= 5)
            def _(h=h, k=k):
                across = jnp.where(h == 1, 2, -2)
                message(h, k, jnp.where(k == 7, across, jnp.where(k == 5, 1, -1))).start()

        for k, others, first, heads in joins:
            mine = g == first + heads[0]
            for h in heads[1:]:
                mine = mine | (g == first + h)

            @pl.when(mine)
            def _(k=k, others=others, first=first):
                pass_on(g - first, k, 1 if k % 2 else -1, others)

        return carry

    lax.fori_loop(0, UNITS // 2 - 1, turn, 0)
    work(jnp.int32(UNITS // 2 - 1), last=True)

    def written(h):
        columns = pl.ds(h * HD, HD)
        return [
            pltpu.make_async_copy(held.at[:, columns], out.at[:, columns], w_sem.at[h, i])
            for i, (held, out) in enumerate(((s_out, s_hbm), (t_out, t_hbm)))
        ]

    for h in range(HEADS_DEV):
        for k in (1, 2):
            arrived(h, k)
        final = []
        for i in range(2):
            out, _, total = merge(
                [unpack(outbox, h, 0, i)] + [unpack(inbox, h, k, i) for k in (1, 2)]
            )
            final.append((out / total).astype(BF))
        s_out[:, h * HD:(h + 1) * HD] = final[0]
        t_out[:, h * HD:(h + 1) * HD] = final[1]
        apart = final[1].astype(F32) - final[0].astype(F32)
        gap_sum[...] += apart * apart
        for copy in written(h):
            copy.start()

    tall = jnp.concatenate([gap_sum[...], jnp.zeros((2 * HD - ROWS, HD), F32)], axis=0)
    gap_in[head] = jnp.broadcast_to(jnp.sum(tall.T, axis=0, keepdims=True), (8, 2 * HD))

    def gap_copy(step, arriving):
        other = lax.rem(head + (PEERS - step if arriving else step), PEERS)
        box = gap_in.at[other if arriving else head]
        return pltpu.make_async_remote_copy(
            src_ref=box,
            dst_ref=box,
            send_sem=d_send.at[step - 1],
            recv_sem=d_recv.at[step - 1],
            device_id={"head": other},
            device_id_type=MESH,
        )

    for step in range(1, PEERS):
        gap_copy(step, False).start()
    for leg in legs:
        leg_copy(leg).wait_send()
    for h in range(HEADS_DEV):
        for k in range(1, RING):
            message(h, k, 1).wait_send()
    for step in range(1, PEERS):
        gap_copy(step, True).wait_recv()
    total = gap_in[0]
    for peer in range(1, PEERS):
        total = total + gap_in[peer]
    gap_out[...] = total / F32(PEERS * HEADS_DEV * HD)
    gap_copied = pltpu.make_async_copy(gap_out, gap_hbm, w_sem.at[HEADS_DEV, 0])
    gap_copied.start()
    for h in range(HEADS_DEV):
        for copy in written(h):
            copy.wait()
    gap_copied.wait()
    for step in range(1, PEERS):
        gap_copy(step, False).wait_send()


def hand_over(s_ref, t_ref, gap_ref, s_out, t_out, gap_out, held, gap_held, sem):
    gap_in = pltpu.make_async_copy(gap_ref, gap_held, sem.at[2, 0])
    ways = []
    for i, (source, target) in enumerate(((s_ref, s_out), (t_ref, t_out))):
        ways.append((
            pltpu.make_async_copy(source, held.at[i], sem.at[i, 0]),
            pltpu.make_async_copy(held.at[i], target, sem.at[i, 1]),
        ))
    for arrive, _ in ways:
        arrive.start()
    gap_in.start()
    for arrive, leave in ways:
        arrive.wait()
        leave.start()
    gap_in.wait()
    gap_out[...] = gap_held[0:1, :ROWS]
    for _, leave in ways:
        leave.wait()


def on_device(queries, keys, values, block_group, group_mask, teacher_gain):
    vmem = pl.BlockSpec(memory_space=pltpu.VMEM)
    outside = pl.BlockSpec(memory_space=pltpu.HBM)
    legs = 31
    student, teacher, gap = pl.pallas_call(
        kernel,
        out_shape=(
            jax.ShapeDtypeStruct((ROWS, HEADS_DEV * HD), BF),
            jax.ShapeDtypeStruct((ROWS, HEADS_DEV * HD), BF),
            jax.ShapeDtypeStruct((8, 2 * HD), F32),
        ),
        in_specs=[outside] * 6,
        out_specs=(outside,) * 3,
        scratch_shapes=[
            pltpu.VMEM((HEADS_DEV, RING, 2, ROWS, HD), BF),
            pltpu.VMEM((RING, HEADS_DEV, ROWS, HD), BF),
            pltpu.SMEM(block_group.shape, jnp.int32),
            pltpu.SMEM(group_mask.shape, jnp.int32),
            pltpu.VMEM(teacher_gain.shape, F32),
            pltpu.VMEM((RING, 8, KEYS), F32),
            pltpu.VMEM((HEADS_DEV, 8, HD), F32),
            pltpu.VMEM((2 * ROWS, KEYS), F32),
            pltpu.VMEM((2 * ROWS, KEYS), F32),
            pltpu.VMEM((ROWS, HEADS_DEV * HD), BF),
            pltpu.VMEM((ROWS, HEADS_DEV * HD), BF),
            pltpu.VMEM((8, 2 * HD), F32),
            pltpu.VMEM((HEADS_DEV, RING, ROWS + STAT, 2 * HD), BF),
            pltpu.VMEM((HEADS_DEV, RING, ROWS + STAT, 2 * HD), BF),
            pltpu.VMEM((ROWS, HD), F32),
            pltpu.VMEM((PEERS, 8, 2 * HD), F32),
            pltpu.SemaphoreType.DMA((HEADS_DEV + 1, 3)),
            pltpu.SemaphoreType.DMA((HEADS_DEV + 1, 2)),
            pltpu.SemaphoreType.DMA((legs,)),
            pltpu.SemaphoreType.DMA((legs,)),
            pltpu.SemaphoreType.DMA((HEADS_DEV, RING)),
            pltpu.SemaphoreType.DMA((HEADS_DEV, RING)),
            pltpu.SemaphoreType.DMA((PEERS - 1,)),
            pltpu.SemaphoreType.DMA((PEERS - 1,)),
        ],
        compiler_params=pltpu.CompilerParams(
            collective_id=0, has_side_effects=True, vmem_limit_bytes=64 * 2**20
        ),
    )(queries, keys, values, block_group, group_mask, teacher_gain)
    student, teacher, gap = pl.pallas_call(
        hand_over,
        out_shape=(
            jax.ShapeDtypeStruct(student.shape, BF),
            jax.ShapeDtypeStruct(teacher.shape, BF),
            jax.ShapeDtypeStruct((1, ROWS), F32),
        ),
        in_specs=[outside] * 3,
        out_specs=(outside, outside, vmem),
        scratch_shapes=[
            pltpu.VMEM((2, ROWS, HEADS_DEV * HD), BF),
            pltpu.VMEM((8, 2 * HD), F32),
            pltpu.SemaphoreType.DMA((3, 2)),
        ],
        compiler_params=pltpu.CompilerParams(vmem_limit_bytes=64 * 2**20),
    )(student, teacher, gap)
    return student, teacher, gap.reshape(ROWS)


def solution(mesh):
    placed = (P("tm", "head"), P("tm", "head"), P("tm", "head"), P(), P(), P("head"))
    return jax.shard_map(
        on_device,
        mesh=mesh,
        in_specs=placed,
        out_specs=(P("tm", "head"), P("tm", "head"), P("tm")),
        check_vma=False,
    )
```

```python
import functools
import math

import jax
import jax.numpy as jnp
from jax import lax
from jax.experimental import pallas as pl
from jax.experimental.pallas import tpu as pltpu
from jax.sharding import PartitionSpec as P

HD = 128
RING = 8
HEADS_DEV = 3
PEERS = 8
ROWS = 160
STAT = 16
KEYS = RING * ROWS
UNITS = RING * HEADS_DEV
SCALE = math.log2(math.e) / math.sqrt(HD)
EMPTY = -(2.0**100)
MESH = pl.DeviceIdType.MESH
NT = (((1,), (1,)), ((), ()))
TN = (((0,), (0,)), ((), ()))
BF = jnp.bfloat16
F32 = jnp.float32


def kernel(
    q_ref, k_ref, v_ref, group_ref, mask_ref, gain_ref,
    s_hbm, t_hbm, gap_hbm,
    kv_all, q_all, group_all, mask_all, gain_all, bias, gains, score0, score1, s_out, t_out, gap_out, inbox, outbox, gap_sum, gap_in,
    l_sem, w_sem, g_send, g_recv, o_send, o_recv, d_send, d_recv,
):
    tm = lax.axis_index("tm")
    head = lax.axis_index("head")
    core = lax.rem(head, 2)
    zpos, ypos = lax.div(tm, RING), lax.rem(tm, RING)
    kpos = jnp.where(core == 0, zpos, ypos)
    qpos = jnp.where(core == 0, ypos, zpos)

    def device(kp, qp):
        return jnp.where(core == 0, kp * RING + qp, qp * RING + kp)

    def wrap(x):
        return lax.rem(x + 2 * RING, RING)

    def k_device(shift):
        return device(wrap(kpos + shift), qpos)

    def q_device(shift):
        return device(kpos, wrap(qpos + shift))

    sources = (q_ref, k_ref, v_ref)
    own_copies = []
    for h in range(HEADS_DEV):
        places = (q_all.at[0, h], kv_all.at[h, 0, 0], kv_all.at[h, 0, 1])
        for i, (source, place) in enumerate(zip(sources, places)):
            own_copies.append(
                pltpu.make_async_copy(source.at[:, pl.ds(h * HD, HD)], place, l_sem.at[h, i])
            )
    small = ((group_ref, group_all), (mask_ref, mask_all), (gain_ref, gain_all))
    small_copies = [
        pltpu.make_async_copy(source, place, l_sem.at[HEADS_DEV, i])
        for i, (source, place) in enumerate(small)
    ]
    barrier = pltpu.get_barrier_semaphore()
    nears = [k_device(1), k_device(-1)] + [q_device(shift) for shift in (1, -1, 2, -2)]
    for near in nears:
        pl.semaphore_signal(barrier, inc=1, device_id={"tm": near}, device_id_type=MESH)
    for step in range(1, PEERS):
        pl.semaphore_signal(
            barrier, inc=1, device_id={"head": lax.rem(head + step, PEERS)}, device_id_type=MESH
        )

    def number(way, far):
        return 0 if far == 0 else 7 if far == 4 else 2 * far - (way > 0)

    def offset(k):
        return jnp.where(lax.rem(k, 2) == 1, lax.div(k + 1, 2), -lax.div(k, 2))

    legs = [(what, way, hop) for hop in (1, 2, 3) for what in (0, "q", 1, 2) for way in (1, -1)]
    legs += [(what, way, 4) for what in (0, "q", 1, 2) for way in (1, -1)]

    def leg_copy(leg):
        what, way, hop = leg
        here, there = number(-way, hop - 1), number(-way, hop)
        if what == "q":
            ends = q_all.at[here], q_all.at[there]
            if hop == 4:
                heads = pl.ds(0, 1) if way == 1 else pl.ds(1, HEADS_DEV - 1)
                ends = tuple(end.at[heads] for end in ends)
            near = q_device(way)
        else:
            ends = kv_all.at[what, here], kv_all.at[what, there]
            if hop == 4:
                half = 0 if way == 1 else 1
                ends = tuple(end.at[half] for end in ends)
            near = k_device(way)
        i = legs.index(leg)
        return pltpu.make_async_remote_copy(
            src_ref=ends[0],
            dst_ref=ends[1],
            send_sem=g_send.at[i],
            recv_sem=g_recv.at[i],
            device_id={"tm": near},
            device_id_type=MESH,
        )

    def send_own(leg):
        what, way, _ = leg
        i = legs.index(leg)
        if what == "q":
            pieces = [(q_ref, h, q_all.at[number(-way, 1), h]) for h in range(HEADS_DEV)]
        else:
            pieces = [
                (source, what, kv_all.at[what, number(-way, 1), half])
                for half, source in enumerate((k_ref, v_ref))
            ]
        for source, h, place in pieces:
            pltpu.make_async_remote_copy(
                src_ref=source.at[:, pl.ds(h * HD, HD)],
                dst_ref=place,
                send_sem=g_send.at[i],
                recv_sem=g_recv.at[i],
                device_id={"tm": (q_device if what == "q" else k_device)(way)},
                device_id_type=MESH,
            ).start()

    def relay(hop):
        for leg in legs:
            if leg[2] == hop:
                leg_copy(leg).wait_recv()
                onward = (leg[0], leg[1], hop + 1)
                if onward in legs:
                    leg_copy(onward).start()

    def wait_last(what, ways=(1, -1)):
        for leg in legs:
            if leg[0] == what and leg[1] in ways and leg[2] == 4:
                leg_copy(leg).wait_recv()

    pl.semaphore_wait(barrier, len(nears) + PEERS - 1)
    for leg in legs:
        if leg[2] == 1:
            send_own(leg)
    for copy in small_copies + own_copies:
        copy.start()

    for copy in small_copies:
        copy.wait()
    for h in range(HEADS_DEV):
        gains[h] = jnp.broadcast_to(gain_all[h * HD:(h + 1) * HD][None, :], (8, HD))
    gap_sum[...] = jnp.zeros((ROWS, HD), F32)

    def set_bias(k, carry):
        q_group = group_all[device(kpos, wrap(qpos + offset(k)))]
        block_of = lax.div(lax.broadcasted_iota(jnp.int32, (8, KEYS), 1), ROWS)
        row = jnp.zeros((8, KEYS), F32)
        for i in range(RING):
            step = (i + 1) // 2 if i % 2 else -(i // 2)
            keep = mask_all[q_group, group_all[k_device(step)]]
            row = jnp.where(block_of == i, jnp.where(keep == 1, F32(0.0), F32(EMPTY)), row)
        bias[k] = row
        return carry

    lax.fori_loop(0, RING, set_bias, 0)

    for hop in (1, 2, 3):
        relay(hop)
    for copy in own_copies:
        copy.wait()
    wait_last(0)

    def scores(h, k, score):
        queries = q_all[k, h]
        gain = gains[h][0:1, :]
        teacher = (queries.astype(F32) * gain).astype(BF)
        both = jnp.concatenate([queries, teacher], axis=0)
        keys = kv_all[h, :, 0].reshape(KEYS, HD)
        score[...] = lax.dot_general(both, keys, NT, preferred_element_type=F32)

    def mix(h, k, score):
        s = jnp.concatenate([score[:ROWS, :] + bias[k][0:1, :], score[ROWS:, :]], axis=0)
        shift = jnp.max(s, axis=-1, keepdims=True).astype(BF).astype(F32)
        weight = jnp.exp2((s - shift) * SCALE).astype(BF)
        right = jnp.concatenate(
            [kv_all[h, :, 1].reshape(KEYS, HD), jnp.ones((KEYS, HD), BF)], axis=1
        )
        mixed = jnp.dot(weight, right, preferred_element_type=F32)
        shift = jnp.broadcast_to(shift, (2 * ROWS, HD))
        halves = (slice(0, ROWS), slice(ROWS, 2 * ROWS))
        pack(h, k, [(mixed[half, :HD], shift[half], mixed[half, HD:]) for half in halves])

    def unit(u):
        far = u - 3
        middle = u - 9
        near = u - 15
        last = lax.rem(far + 3, 3)
        h = jnp.where(
            u < 3, 0,
            jnp.where(
                u < 9, 1 + lax.div(far, 3),
                jnp.where(u < 15, lax.div(middle, 2), jnp.where(u < 21, lax.div(near, 2), u - 21)),
            ),
        )
        k = jnp.where(
            u < 3, 5 + u,
            jnp.where(
                u < 9, jnp.where(last == 0, 7, 4 + last),
                jnp.where(
                    u < 15, 3 + lax.rem(middle, 2), jnp.where(u < 21, 1 + lax.rem(near, 2), 0)
                ),
            ),
        )
        return h, k

    stat_lane = lax.broadcasted_iota(jnp.int32, (ROWS, HD), 1)
    stat_row = lax.broadcasted_iota(jnp.int32, (STAT, 2 * HD), 0)
    sum_side = jnp.where(lax.broadcasted_iota(jnp.int32, (STAT, 2 * HD), 1) >= HD, 1, 0)
    wanted = [lax.div(stat_row - 3 * i + 1, 2) for i in range(2)]
    spread = [
        jnp.where((wanted[i] == sum_side) & (stat_row >= 3 * i), F32(1.0), F32(0.0)).astype(BF)
        for i in range(2)
    ]

    def unpack(box, h, k, i):
        out = box[h, k, :ROWS, i * HD:(i + 1) * HD].astype(F32)
        stat = lax.dot_general(
            box[h, k, ROWS:, :ROWS], spread[i], TN, preferred_element_type=F32
        )
        return out, stat[:, :HD], stat[:, HD:]

    def merge(parts):
        top = parts[0][1]
        for _, shift, _ in parts[1:]:
            top = jnp.maximum(top, shift)
        mixed = 0.0
        total = 0.0
        for out, shift, weight in parts:
            share = jnp.exp2((shift - top) * SCALE)
            mixed = mixed + share * out
            total = total + share * weight
        return mixed, top, total

    def message(h, k, shift):
        return pltpu.make_async_remote_copy(
            src_ref=outbox.at[h, k],
            dst_ref=inbox.at[h, k],
            send_sem=o_send.at[h, k],
            recv_sem=o_recv.at[h, k],
            device_id={"tm": q_device(shift)},
            device_id_type=MESH,
        )

    def arrived(h, k):
        message(h, k, 1).wait_recv()

    def pack(h, k, parts):
        packed = jnp.zeros((ROWS, HD), F32)
        for i, (out, shift, weight) in enumerate(parts):
            outbox[h, k, :ROWS, i * HD:(i + 1) * HD] = out.astype(BF)
            upper = weight.astype(BF).astype(F32)
            for piece, value in enumerate((shift, upper, weight - upper)):
                packed = jnp.where(stat_lane == 3 * i + piece, value, packed)
        packed = jnp.concatenate([packed, jnp.zeros((2 * HD - ROWS, HD), F32)], axis=0)
        outbox[h, k, ROWS:, :] = packed.T[:STAT].astype(BF)

    def pass_on(h, k, shift, others):
        for other in others:
            arrived(h, other)
        pack(h, k, [
            merge([unpack(outbox, h, k, i)] + [unpack(inbox, h, other, i) for other in others])
            for i in range(2)
        ])
        message(h, k, shift).start()

    def work(g, last=False):
        h0, k0 = unit(2 * g)
        h1, k1 = unit(2 * g + 1)
        scores(h1, k1, score1)
        mix(h0, k0, score0)
        if not last:
            h2, k2 = unit(2 * g + 2)
            scores(h2, k2, score0)
        mix(h1, k1, score1)
        return (h0, k0), (h1, k1)

    scores(0, 5, score0)

    joins = ((3, (5,), 4, (0, 2)), (3, (5, 7), 4, (1,)), (4, (6, 7), 5, (0, 2)), (4, (6,), 5, (1,)))
    joins += ((1, (3,), 7, (0, 1, 2)), (2, (4,), 8, (0, 1, 2)))

    def turn(g, carry):
        for when, what, ways in ((0, "q", (1,)), (1, "q", (-1,)), (1, 1, (1, -1)), (2, 2, (1, -1))):
            @pl.when(g == when)
            def _(what=what, ways=ways):
                wait_last(what, ways)

        for h, k in work(g):
            @pl.when(k >= 5)
            def _(h=h, k=k):
                across = jnp.where(h == 1, 2, -2)
                message(h, k, jnp.where(k == 7, across, jnp.where(k == 5, 1, -1))).start()

        for k, others, first, heads in joins:
            mine = g == first + heads[0]
            for h in heads[1:]:
                mine = mine | (g == first + h)

            @pl.when(mine)
            def _(k=k, others=others, first=first):
                pass_on(g - first, k, 1 if k % 2 else -1, others)

        return carry

    lax.fori_loop(0, UNITS // 2 - 1, turn, 0)
    work(jnp.int32(UNITS // 2 - 1), last=True)

    def written(h):
        columns = pl.ds(h * HD, HD)
        return [
            pltpu.make_async_copy(held.at[:, columns], out.at[:, columns], w_sem.at[h, i])
            for i, (held, out) in enumerate(((s_out, s_hbm), (t_out, t_hbm)))
        ]

    for h in range(HEADS_DEV):
        for k in (1, 2):
            arrived(h, k)
        final = []
        for i in range(2):
            out, _, total = merge(
                [unpack(outbox, h, 0, i)] + [unpack(inbox, h, k, i) for k in (1, 2)]
            )
            final.append((out / total).astype(BF))
        s_out[:, h * HD:(h + 1) * HD] = final[0]
        t_out[:, h * HD:(h + 1) * HD] = final[1]
        apart = final[1].astype(F32) - final[0].astype(F32)
        gap_sum[...] += apart * apart
        for copy in written(h):
            copy.start()

    tall = jnp.concatenate([gap_sum[...], jnp.zeros((2 * HD - ROWS, HD), F32)], axis=0)
    gap_in[head] = jnp.broadcast_to(jnp.sum(tall.T, axis=0, keepdims=True), (8, 2 * HD))

    def gap_copy(step, arriving):
        other = lax.rem(head + (PEERS - step if arriving else step), PEERS)
        box = gap_in.at[other if arriving else head]
        return pltpu.make_async_remote_copy(
            src_ref=box,
            dst_ref=box,
            send_sem=d_send.at[step - 1],
            recv_sem=d_recv.at[step - 1],
            device_id={"head": other},
            device_id_type=MESH,
        )

    for step in range(1, PEERS):
        gap_copy(step, False).start()
    for leg in legs:
        leg_copy(leg).wait_send()
    for h in range(HEADS_DEV):
        for k in range(1, RING):
            message(h, k, 1).wait_send()
    for step in range(1, PEERS):
        gap_copy(step, True).wait_recv()
    total = gap_in[0]
    for peer in range(1, PEERS):
        total = total + gap_in[peer]
    gap_out[...] = total / F32(PEERS * HEADS_DEV * HD)
    gap_copied = pltpu.make_async_copy(gap_out, gap_hbm, w_sem.at[HEADS_DEV, 0])
    gap_copied.start()
    for h in range(HEADS_DEV):
        for copy in written(h):
            copy.wait()
    gap_copied.wait()
    for step in range(1, PEERS):
        gap_copy(step, False).wait_send()


def hand_over(s_ref, t_ref, gap_ref, s_out, t_out, gap_out, held, gap_held, sem):
    gap_in = pltpu.make_async_copy(gap_ref, gap_held, sem.at[2, 0])
    ways = []
    for i, (source, target) in enumerate(((s_ref, s_out), (t_ref, t_out))):
        ways.append((
            pltpu.make_async_copy(source, held.at[i], sem.at[i, 0]),
            pltpu.make_async_copy(held.at[i], target, sem.at[i, 1]),
        ))
    for arrive, _ in ways:
        arrive.start()
    gap_in.start()
    for arrive, leave in ways:
        arrive.wait()
        leave.start()
    gap_in.wait()
    gap_out[...] = gap_held[0:1, :ROWS]
    for _, leave in ways:
        leave.wait()


def on_device(queries, keys, values, block_group, group_mask, teacher_gain):
    vmem = pl.BlockSpec(memory_space=pltpu.VMEM)
    outside = pl.BlockSpec(memory_space=pltpu.HBM)
    legs = 32
    student, teacher, gap = pl.pallas_call(
        kernel,
        out_shape=(
            jax.ShapeDtypeStruct((ROWS, HEADS_DEV * HD), BF),
            jax.ShapeDtypeStruct((ROWS, HEADS_DEV * HD), BF),
            jax.ShapeDtypeStruct((8, 2 * HD), F32),
        ),
        in_specs=[outside] * 6,
        out_specs=(outside,) * 3,
        scratch_shapes=[
            pltpu.VMEM((HEADS_DEV, RING, 2, ROWS, HD), BF),
            pltpu.VMEM((RING, HEADS_DEV, ROWS, HD), BF),
            pltpu.SMEM(block_group.shape, jnp.int32),
            pltpu.SMEM(group_mask.shape, jnp.int32),
            pltpu.VMEM(teacher_gain.shape, F32),
            pltpu.VMEM((RING, 8, KEYS), F32),
            pltpu.VMEM((HEADS_DEV, 8, HD), F32),
            pltpu.VMEM((2 * ROWS, KEYS), F32),
            pltpu.VMEM((2 * ROWS, KEYS), F32),
            pltpu.VMEM((ROWS, HEADS_DEV * HD), BF),
            pltpu.VMEM((ROWS, HEADS_DEV * HD), BF),
            pltpu.VMEM((8, 2 * HD), F32),
            pltpu.VMEM((HEADS_DEV, RING, ROWS + STAT, 2 * HD), BF),
            pltpu.VMEM((HEADS_DEV, RING, ROWS + STAT, 2 * HD), BF),
            pltpu.VMEM((ROWS, HD), F32),
            pltpu.VMEM((PEERS, 8, 2 * HD), F32),
            pltpu.SemaphoreType.DMA((HEADS_DEV + 1, 3)),
            pltpu.SemaphoreType.DMA((HEADS_DEV + 1, 2)),
            pltpu.SemaphoreType.DMA((legs,)),
            pltpu.SemaphoreType.DMA((legs,)),
            pltpu.SemaphoreType.DMA((HEADS_DEV, RING)),
            pltpu.SemaphoreType.DMA((HEADS_DEV, RING)),
            pltpu.SemaphoreType.DMA((PEERS - 1,)),
            pltpu.SemaphoreType.DMA((PEERS - 1,)),
        ],
        compiler_params=pltpu.CompilerParams(
            collective_id=0, has_side_effects=True, vmem_limit_bytes=64 * 2**20
        ),
    )(queries, keys, values, block_group, group_mask, teacher_gain)
    student, teacher, gap = pl.pallas_call(
        hand_over,
        out_shape=(
            jax.ShapeDtypeStruct(student.shape, BF),
            jax.ShapeDtypeStruct(teacher.shape, BF),
            jax.ShapeDtypeStruct((1, ROWS), F32),
        ),
        in_specs=[outside] * 3,
        out_specs=(outside, outside, vmem),
        scratch_shapes=[
            pltpu.VMEM((2, ROWS, HEADS_DEV * HD), BF),
            pltpu.VMEM((8, 2 * HD), F32),
            pltpu.SemaphoreType.DMA((3, 2)),
        ],
        compiler_params=pltpu.CompilerParams(vmem_limit_bytes=64 * 2**20),
    )(student, teacher, gap)
    return student, teacher, gap.reshape(ROWS)


def solution(mesh):
    placed = (P("tm", "head"), P("tm", "head"), P("tm", "head"), P(), P(), P("head"))
    return jax.shard_map(
        on_device,
        mesh=mesh,
        in_specs=placed,
        out_specs=(P("tm", "head"), P("tm", "head"), P("tm")),
        check_vma=False,
    )
```

```python
import functools
import math

import jax
import jax.numpy as jnp
from jax import lax
from jax.experimental import pallas as pl
from jax.experimental.pallas import tpu as pltpu
from jax.sharding import PartitionSpec as P

HD = 128
RING = 8
HEADS_DEV = 3
PEERS = 8
ROWS = 160
STAT = 16
KEYS = RING * ROWS
UNITS = RING * HEADS_DEV
SCALE = math.log2(math.e) / math.sqrt(HD)
EMPTY = -(2.0**100)
MESH = pl.DeviceIdType.MESH
NT = (((1,), (1,)), ((), ()))
TN = (((0,), (0,)), ((), ()))
BF = jnp.bfloat16
F32 = jnp.float32


def kernel(
    q_ref, k_ref, v_ref, group_ref, mask_ref, gain_ref,
    s_hbm, t_hbm, gap_hbm,
    kv_all, q_all, group_all, mask_all, gain_all, bias, gains, score0, score1, s_out, t_out, gap_out, inbox, outbox, gap_sum, gap_in,
    l_sem, w_sem, g_send, g_recv, o_send, o_recv, d_send, d_recv,
):
    tm = lax.axis_index("tm")
    head = lax.axis_index("head")
    core = lax.rem(head, 2)
    zpos, ypos = lax.div(tm, RING), lax.rem(tm, RING)
    kpos = jnp.where(core == 0, zpos, ypos)
    qpos = jnp.where(core == 0, ypos, zpos)

    def device(kp, qp):
        return jnp.where(core == 0, kp * RING + qp, qp * RING + kp)

    def wrap(x):
        return lax.rem(x + 2 * RING, RING)

    def k_device(shift):
        return device(wrap(kpos + shift), qpos)

    def q_device(shift):
        return device(kpos, wrap(qpos + shift))

    sources = (q_ref, k_ref, v_ref)
    own_copies = []
    for h in range(HEADS_DEV):
        places = (q_all.at[0, h], kv_all.at[h, 0, 0], kv_all.at[h, 0, 1])
        for i, (source, place) in enumerate(zip(sources, places)):
            own_copies.append(
                pltpu.make_async_copy(source.at[:, pl.ds(h * HD, HD)], place, l_sem.at[h, i])
            )
    small = ((group_ref, group_all), (mask_ref, mask_all), (gain_ref, gain_all))
    small_copies = [
        pltpu.make_async_copy(source, place, l_sem.at[HEADS_DEV, i])
        for i, (source, place) in enumerate(small)
    ]
    barrier = pltpu.get_barrier_semaphore()
    nears = [k_device(1), k_device(-1)] + [q_device(shift) for shift in (1, -1, 2, -2)]
    for near in nears:
        pl.semaphore_signal(barrier, inc=1, device_id={"tm": near}, device_id_type=MESH)
    for step in range(1, PEERS):
        pl.semaphore_signal(
            barrier, inc=1, device_id={"head": lax.rem(head + step, PEERS)}, device_id_type=MESH
        )

    def number(way, far):
        return 0 if far == 0 else 7 if far == 4 else 2 * far - (way > 0)

    def offset(k):
        return jnp.where(lax.rem(k, 2) == 1, lax.div(k + 1, 2), -lax.div(k, 2))

    legs = [(what, way, hop) for hop in (1, 2, 3) for what in (0, "q", 1, 2) for way in (1, -1)]
    legs += [(what, way, 4) for what in (0, "q", 1, 2) for way in (1, -1)]

    def leg_copy(leg):
        what, way, hop = leg
        here, there = number(-way, hop - 1), number(-way, hop)
        if what == "q":
            ends = q_all.at[here], q_all.at[there]
            if hop == 4:
                heads = pl.ds(0, 1) if way == 1 else pl.ds(1, HEADS_DEV - 1)
                ends = tuple(end.at[heads] for end in ends)
            near = q_device(way)
        else:
            ends = kv_all.at[what, here], kv_all.at[what, there]
            if hop == 4:
                half = 0 if way == 1 else 1
                ends = tuple(end.at[half] for end in ends)
            near = k_device(way)
        i = legs.index(leg)
        return pltpu.make_async_remote_copy(
            src_ref=ends[0],
            dst_ref=ends[1],
            send_sem=g_send.at[i],
            recv_sem=g_recv.at[i],
            device_id={"tm": near},
            device_id_type=MESH,
        )

    def send_own(leg):
        what, way, _ = leg
        i = legs.index(leg)
        if what == "q":
            pieces = [(q_ref, h, q_all.at[number(-way, 1), h]) for h in range(HEADS_DEV)]
        else:
            pieces = [
                (source, what, kv_all.at[what, number(-way, 1), half])
                for half, source in enumerate((k_ref, v_ref))
            ]
        for source, h, place in pieces:
            pltpu.make_async_remote_copy(
                src_ref=source.at[:, pl.ds(h * HD, HD)],
                dst_ref=place,
                send_sem=g_send.at[i],
                recv_sem=g_recv.at[i],
                device_id={"tm": (q_device if what == "q" else k_device)(way)},
                device_id_type=MESH,
            ).start()

    def relay(hop):
        for leg in legs:
            if leg[2] == hop:
                leg_copy(leg).wait_recv()
                onward = (leg[0], leg[1], hop + 1)
                if onward in legs:
                    leg_copy(onward).start()

    def wait_last(what, ways=(1, -1)):
        for leg in legs:
            if leg[0] == what and leg[1] in ways and leg[2] == 4:
                leg_copy(leg).wait_recv()

    pl.semaphore_wait(barrier, len(nears) + PEERS - 1)
    for leg in legs:
        if leg[2] == 1:
            send_own(leg)
    for copy in small_copies + own_copies:
        copy.start()

    for copy in small_copies:
        copy.wait()
    for h in range(HEADS_DEV):
        gains[h] = jnp.broadcast_to(gain_all[h * HD:(h + 1) * HD][None, :], (8, HD))
    gap_sum[...] = jnp.zeros((ROWS, HD), F32)

    def set_bias(k, carry):
        q_group = group_all[device(kpos, wrap(qpos + offset(k)))]
        block_of = lax.div(lax.broadcasted_iota(jnp.int32, (8, KEYS), 1), ROWS)
        row = jnp.zeros((8, KEYS), F32)
        for i in range(RING):
            step = (i + 1) // 2 if i % 2 else -(i // 2)
            keep = mask_all[q_group, group_all[k_device(step)]]
            row = jnp.where(block_of == i, jnp.where(keep == 1, F32(0.0), F32(EMPTY)), row)
        bias[k] = row
        return carry

    lax.fori_loop(0, RING, set_bias, 0)

    for hop in (1, 2, 3):
        relay(hop)
    for copy in own_copies:
        copy.wait()
    wait_last(0)

    def scores(h, k, score):
        queries = q_all[k, h]
        gain = gains[h][0:1, :]
        teacher = (queries.astype(F32) * gain).astype(BF)
        both = jnp.concatenate([queries, teacher], axis=0)
        keys = kv_all[h, :, 0].reshape(KEYS, HD)
        score[...] = lax.dot_general(both, keys, NT, preferred_element_type=F32)

    def mix(h, k, score):
        s = jnp.concatenate([score[:ROWS, :] + bias[k][0:1, :], score[ROWS:, :]], axis=0)
        shift = jnp.max(s, axis=-1, keepdims=True).astype(BF).astype(F32)
        weight = jnp.exp2((s - shift) * SCALE).astype(BF)
        right = jnp.concatenate(
            [kv_all[h, :, 1].reshape(KEYS, HD), jnp.ones((KEYS, HD), BF)], axis=1
        )
        mixed = jnp.dot(weight, right, preferred_element_type=F32)
        shift = jnp.broadcast_to(shift, (2 * ROWS, HD))
        halves = (slice(0, ROWS), slice(ROWS, 2 * ROWS))
        pack(h, k, [(mixed[half, :HD], shift[half], mixed[half, HD:]) for half in halves])

    def unit(u):
        far = u - 3
        middle = u - 9
        near = u - 15
        last = lax.rem(far + 3, 3)
        h = jnp.where(
            u < 3, 0,
            jnp.where(
                u < 9, 1 + lax.div(far, 3),
                jnp.where(u < 15, lax.div(middle, 2), jnp.where(u < 21, lax.div(near, 2), u - 21)),
            ),
        )
        k = jnp.where(
            u < 3, 5 + u,
            jnp.where(
                u < 9, jnp.where(last == 0, 7, 4 + last),
                jnp.where(
                    u < 15, 3 + lax.rem(middle, 2), jnp.where(u < 21, 1 + lax.rem(near, 2), 0)
                ),
            ),
        )
        return h, k

    stat_lane = lax.broadcasted_iota(jnp.int32, (ROWS, HD), 1)
    stat_row = lax.broadcasted_iota(jnp.int32, (STAT, 2 * HD), 0)
    sum_side = jnp.where(lax.broadcasted_iota(jnp.int32, (STAT, 2 * HD), 1) >= HD, 1, 0)
    wanted = [lax.div(stat_row - 3 * i + 1, 2) for i in range(2)]
    spread = [
        jnp.where((wanted[i] == sum_side) & (stat_row >= 3 * i), F32(1.0), F32(0.0)).astype(BF)
        for i in range(2)
    ]

    def unpack(box, h, k, i):
        out = box[h, k, :ROWS, i * HD:(i + 1) * HD].astype(F32)
        stat = lax.dot_general(
            box[h, k, ROWS:, :ROWS], spread[i], TN, preferred_element_type=F32
        )
        return out, stat[:, :HD], stat[:, HD:]

    def merge(parts):
        top = parts[0][1]
        for _, shift, _ in parts[1:]:
            top = jnp.maximum(top, shift)
        mixed = 0.0
        total = 0.0
        for out, shift, weight in parts:
            share = jnp.exp2((shift - top) * SCALE)
            mixed = mixed + share * out
            total = total + share * weight
        return mixed, top, total

    def message(h, k, shift):
        return pltpu.make_async_remote_copy(
            src_ref=outbox.at[h, k],
            dst_ref=inbox.at[h, k],
            send_sem=o_send.at[h, k],
            recv_sem=o_recv.at[h, k],
            device_id={"tm": q_device(shift)},
            device_id_type=MESH,
        )

    def arrived(h, k):
        message(h, k, 1).wait_recv()

    def pack(h, k, parts):
        packed = jnp.zeros((ROWS, HD), F32)
        for i, (out, shift, weight) in enumerate(parts):
            outbox[h, k, :ROWS, i * HD:(i + 1) * HD] = out.astype(BF)
            upper = weight.astype(BF).astype(F32)
            for piece, value in enumerate((shift, upper, weight - upper)):
                packed = jnp.where(stat_lane == 3 * i + piece, value, packed)
        packed = jnp.concatenate([packed, jnp.zeros((2 * HD - ROWS, HD), F32)], axis=0)
        outbox[h, k, ROWS:, :] = packed.T[:STAT].astype(BF)

    def pass_on(h, k, shift, others):
        for other in others:
            arrived(h, other)
        pack(h, k, [
            merge([unpack(outbox, h, k, i)] + [unpack(inbox, h, other, i) for other in others])
            for i in range(2)
        ])
        message(h, k, shift).start()

    def send_far(h, k):
        @pl.when(k >= 5)
        def _():
            across = jnp.where(h == 1, 2, -2)
            message(h, k, jnp.where(k == 7, across, jnp.where(k == 5, 1, -1))).start()

    def work(g, last=False):
        h0, k0 = unit(2 * g)
        h1, k1 = unit(2 * g + 1)
        scores(h1, k1, score1)
        mix(h0, k0, score0)
        if not last:
            send_far(h0, k0)
            h2, k2 = unit(2 * g + 2)
            scores(h2, k2, score0)
        mix(h1, k1, score1)
        if not last:
            send_far(h1, k1)

    scores(0, 5, score0)

    joins = ((3, (5,), 4, (0, 2)), (3, (5, 7), 4, (1,)), (4, (6, 7), 5, (0, 2)), (4, (6,), 5, (1,)))
    joins += ((1, (3,), 7, (0, 1, 2)), (2, (4,), 8, (0, 1, 2)))

    def turn(g, carry):
        for when, what, ways in ((0, "q", (1,)), (1, "q", (-1,)), (1, 1, (1, -1)), (2, 2, (1, -1))):
            @pl.when(g == when)
            def _(what=what, ways=ways):
                wait_last(what, ways)

        work(g)

        for k, others, first, heads in joins:
            mine = g == first + heads[0]
            for h in heads[1:]:
                mine = mine | (g == first + h)

            @pl.when(mine)
            def _(k=k, others=others, first=first):
                pass_on(g - first, k, 1 if k % 2 else -1, others)

        return carry

    lax.fori_loop(0, UNITS // 2 - 1, turn, 0)
    work(jnp.int32(UNITS // 2 - 1), last=True)

    def written(h):
        columns = pl.ds(h * HD, HD)
        return [
            pltpu.make_async_copy(held.at[:, columns], out.at[:, columns], w_sem.at[h, i])
            for i, (held, out) in enumerate(((s_out, s_hbm), (t_out, t_hbm)))
        ]

    for h in range(HEADS_DEV):
        for k in (1, 2):
            arrived(h, k)
        final = []
        for i in range(2):
            out, _, total = merge(
                [unpack(outbox, h, 0, i)] + [unpack(inbox, h, k, i) for k in (1, 2)]
            )
            final.append((out / total).astype(BF))
        s_out[:, h * HD:(h + 1) * HD] = final[0]
        t_out[:, h * HD:(h + 1) * HD] = final[1]
        apart = final[1].astype(F32) - final[0].astype(F32)
        gap_sum[...] += apart * apart
        for copy in written(h):
            copy.start()

    tall = jnp.concatenate([gap_sum[...], jnp.zeros((2 * HD - ROWS, HD), F32)], axis=0)
    gap_in[head] = jnp.broadcast_to(jnp.sum(tall.T, axis=0, keepdims=True), (8, 2 * HD))

    def gap_copy(step, arriving):
        other = lax.rem(head + (PEERS - step if arriving else step), PEERS)
        box = gap_in.at[other if arriving else head]
        return pltpu.make_async_remote_copy(
            src_ref=box,
            dst_ref=box,
            send_sem=d_send.at[step - 1],
            recv_sem=d_recv.at[step - 1],
            device_id={"head": other},
            device_id_type=MESH,
        )

    for step in range(1, PEERS):
        gap_copy(step, False).start()
    for leg in legs:
        leg_copy(leg).wait_send()
    for h in range(HEADS_DEV):
        for k in range(1, RING):
            message(h, k, 1).wait_send()
    for step in range(1, PEERS):
        gap_copy(step, True).wait_recv()
    total = gap_in[0]
    for peer in range(1, PEERS):
        total = total + gap_in[peer]
    gap_out[...] = total / F32(PEERS * HEADS_DEV * HD)
    gap_copied = pltpu.make_async_copy(gap_out, gap_hbm, w_sem.at[HEADS_DEV, 0])
    gap_copied.start()
    for h in range(HEADS_DEV):
        for copy in written(h):
            copy.wait()
    gap_copied.wait()
    for step in range(1, PEERS):
        gap_copy(step, False).wait_send()


def hand_over(s_ref, t_ref, gap_ref, s_out, t_out, gap_out, held, gap_held, sem):
    gap_in = pltpu.make_async_copy(gap_ref, gap_held, sem.at[2, 0])
    ways = []
    for i, (source, target) in enumerate(((s_ref, s_out), (t_ref, t_out))):
        ways.append((
            pltpu.make_async_copy(source, held.at[i], sem.at[i, 0]),
            pltpu.make_async_copy(held.at[i], target, sem.at[i, 1]),
        ))
    for arrive, _ in ways:
        arrive.start()
    gap_in.start()
    for arrive, leave in ways:
        arrive.wait()
        leave.start()
    gap_in.wait()
    gap_out[...] = gap_held[0:1, :ROWS]
    for _, leave in ways:
        leave.wait()


def on_device(queries, keys, values, block_group, group_mask, teacher_gain):
    vmem = pl.BlockSpec(memory_space=pltpu.VMEM)
    outside = pl.BlockSpec(memory_space=pltpu.HBM)
    legs = 32
    student, teacher, gap = pl.pallas_call(
        kernel,
        out_shape=(
            jax.ShapeDtypeStruct((ROWS, HEADS_DEV * HD), BF),
            jax.ShapeDtypeStruct((ROWS, HEADS_DEV * HD), BF),
            jax.ShapeDtypeStruct((8, 2 * HD), F32),
        ),
        in_specs=[outside] * 6,
        out_specs=(outside,) * 3,
        scratch_shapes=[
            pltpu.VMEM((HEADS_DEV, RING, 2, ROWS, HD), BF),
            pltpu.VMEM((RING, HEADS_DEV, ROWS, HD), BF),
            pltpu.SMEM(block_group.shape, jnp.int32),
            pltpu.SMEM(group_mask.shape, jnp.int32),
            pltpu.VMEM(teacher_gain.shape, F32),
            pltpu.VMEM((RING, 8, KEYS), F32),
            pltpu.VMEM((HEADS_DEV, 8, HD), F32),
            pltpu.VMEM((2 * ROWS, KEYS), F32),
            pltpu.VMEM((2 * ROWS, KEYS), F32),
            pltpu.VMEM((ROWS, HEADS_DEV * HD), BF),
            pltpu.VMEM((ROWS, HEADS_DEV * HD), BF),
            pltpu.VMEM((8, 2 * HD), F32),
            pltpu.VMEM((HEADS_DEV, RING, ROWS + STAT, 2 * HD), BF),
            pltpu.VMEM((HEADS_DEV, RING, ROWS + STAT, 2 * HD), BF),
            pltpu.VMEM((ROWS, HD), F32),
            pltpu.VMEM((PEERS, 8, 2 * HD), F32),
            pltpu.SemaphoreType.DMA((HEADS_DEV + 1, 3)),
            pltpu.SemaphoreType.DMA((HEADS_DEV + 1, 2)),
            pltpu.SemaphoreType.DMA((legs,)),
            pltpu.SemaphoreType.DMA((legs,)),
            pltpu.SemaphoreType.DMA((HEADS_DEV, RING)),
            pltpu.SemaphoreType.DMA((HEADS_DEV, RING)),
            pltpu.SemaphoreType.DMA((PEERS - 1,)),
            pltpu.SemaphoreType.DMA((PEERS - 1,)),
        ],
        compiler_params=pltpu.CompilerParams(
            collective_id=0, has_side_effects=True, vmem_limit_bytes=64 * 2**20
        ),
    )(queries, keys, values, block_group, group_mask, teacher_gain)
    student, teacher, gap = pl.pallas_call(
        hand_over,
        out_shape=(
            jax.ShapeDtypeStruct(student.shape, BF),
            jax.ShapeDtypeStruct(teacher.shape, BF),
            jax.ShapeDtypeStruct((1, ROWS), F32),
        ),
        in_specs=[outside] * 3,
        out_specs=(outside, outside, vmem),
        scratch_shapes=[
            pltpu.VMEM((2, ROWS, HEADS_DEV * HD), BF),
            pltpu.VMEM((8, 2 * HD), F32),
            pltpu.SemaphoreType.DMA((3, 2)),
        ],
        compiler_params=pltpu.CompilerParams(vmem_limit_bytes=64 * 2**20),
    )(student, teacher, gap)
    return student, teacher, gap.reshape(ROWS)


def solution(mesh):
    placed = (P("tm", "head"), P("tm", "head"), P("tm", "head"), P(), P(), P("head"))
    return jax.shard_map(
        on_device,
        mesh=mesh,
        in_specs=placed,
        out_specs=(P("tm", "head"), P("tm", "head"), P("tm")),
        check_vma=False,
    )
```
